32 devices in a mesh: seq: 8 (over z, y), head: 4 (over x, core).
Axes of the slice: x: 2, y: 2, z: 4, core: 2. Of those that a mesh axis runs over, the one named last changes fastest.
Arguments:
- queries: bfloat16 [28672, 4096], P('seq', 'head'), may hold values from -6 to 6
- key_rows: bfloat16 [28672, 4096], P('seq', 'head'), may hold values from -6 to 6
- value_rows: bfloat16 [28672, 4096], P('seq', 'head'), may hold values from -6 to 6
- band_reach: int32 [112], P('seq'), may hold values from 1 to 3, as said below
- far_list: int32 [112, 2], P('seq'), may hold values from 0 to 111, as said below
- slopes: float32 [32], P('head'), may hold values from 1e-05 to 0.08
Outputs:
- mixed: bfloat16 [28672, 4096], P(('seq', 'head'))
The draws below stay inside these ranges and needn't reach their ends.
Inputs may be any that keep to these rules, and one draw needn't show every extreme that they name: Some query block has band_reach exactly 3. `far_list`: block g lies on index g // 14 of seq. Of the 28 far blocks listed for the query blocks of one index of seq, at most 4 lie on any one index, and exactly 4 on some index.
All inputs are finite; a program needn't handle non-finite values.
Results may differ from the reference program's by a relative error of at most 0.0049.
Values may be sent and summed in bfloat16 or wider, within the bound.
A program may use at most 192 MiB of HBM per device.

```python
import math
import jax
import jax.numpy as jnp
from jax import lax

H = 32
DH = 128
BT = 256
BAND = 3
FAR = 2
BLK_DEV = 14
NBLK = 112
NTOK = 28672
CAP = 4


def drawn(key):
    total_rows = NBLK * BT
    channels = H * DH
    coins = jax.random.randint(jax.random.fold_in(key, 7), (total_rows, channels), 0, 2)
    sign_pattern = (2 * coins - 1).astype(jnp.float32)
    return sign_pattern


def draw_queries(key, part):
    sign_pattern = drawn(key)
    base_draw = jnp.clip(jax.random.normal(jax.random.fold_in(key, 1), sign_pattern.shape, jnp.float32), -6.0, 6.0)
    return base_draw.astype(jnp.bfloat16)


def draw_key_rows(key, part):
    sign_pattern = drawn(key)
    base_draw = jnp.clip(jax.random.normal(jax.random.fold_in(key, 2), sign_pattern.shape, jnp.float32), -6.0, 6.0)
    return base_draw.astype(jnp.bfloat16)


def draw_band_reach(key, part):
    widths = jax.random.randint(jax.random.fold_in(key, 31), (NBLK,), 1, BAND + 1)
    widest = jax.random.randint(jax.random.fold_in(key, 32), (), 0, NBLK)
    return widths.at[widest].set(BAND).astype(jnp.int32)


def far_one_device(device_key):
    device_count = NBLK // BLK_DEV
    request_count = BLK_DEV * FAR
    slot_total = device_count * CAP
    key_heavy, key_order, key_mix, key_local = jax.random.split(device_key, 4)
    heavy = jax.random.randint(key_heavy, (), 0, device_count)
    slot_ids = jnp.arange(slot_total, dtype=jnp.int32)
    slot_source = slot_ids // CAP
    ranking = jax.random.randint(key_order, (slot_total,), 0, 1 << 20) * slot_total + slot_ids
    ranking = jnp.where(slot_source == heavy, slot_ids - 2 * slot_total, ranking)
    order = jnp.argsort(ranking)
    sources = slot_source[order][:request_count]
    mixing = jnp.argsort(jax.random.randint(key_mix, (request_count,), 0, 1 << 20) * request_count + jnp.arange(request_count, dtype=jnp.int32))
    sources = sources[mixing]
    local_blocks = jax.random.randint(key_local, (request_count,), 0, BLK_DEV)
    return (sources * BLK_DEV + local_blocks).reshape(BLK_DEV, FAR)


def draw_far_list(key, part):
    device_count = NBLK // BLK_DEV
    device_keys = jax.random.split(jax.random.fold_in(key, 41), device_count)
    lists = jax.vmap(far_one_device)(device_keys)
    return lists.reshape(NBLK, FAR).astype(jnp.int32)


def levels(stream_key, dims, cuts, smallest, high):
    level, own = 1.0, jax.random.fold_in(stream_key, 6)
    for position, blocks in cuts:
        steps = jnp.exp(jax.random.uniform(jax.random.fold_in(own, position), (blocks,), jnp.float32, smallest / len(cuts), high / len(cuts)))
        level = level * jnp.repeat(steps, dims[position] // blocks).reshape([-1 if axis == position else 1 for axis in range(len(dims))])
    return level


def centred(rng, dims, deviation, bound, cuts=(), kind=jnp.bfloat16):
    values = jax.random.normal(rng, dims, jnp.float32) * deviation
    if len(cuts) > 0:
        values = levels(rng, dims, cuts, -0.22, 0.18) * values
    return jnp.clip(values, min=-bound, max=bound).astype(kind)


def setup_inputs(seed: int = 0) -> dict:
    splits = jax.random.split(jax.random.key(seed), 7)
    queries = draw_queries(jax.random.fold_in(splits[6], 71), 0)
    key_rows = draw_key_rows(jax.random.fold_in(splits[6], 71), 0)
    value_rows = centred(splits[2], (NTOK, H * DH), 1.0, 6.0, ((0, 8), (1, 4)))
    band_reach = draw_band_reach(jax.random.fold_in(splits[6], 71), 0)
    far_list = draw_far_list(jax.random.fold_in(splits[6], 71), 0)
    slopes = jnp.clip(jnp.exp(math.log(0.08) - 8.987197 * jax.random.uniform(splits[5], (H,), jnp.float32) ** levels(splits[5], (H,), ((0, 4),), -0.2, 0.2)), 9.999999747378752e-06, 0.08)
    return {"queries": queries, "key_rows": key_rows, "value_rows": value_rows, "band_reach": band_reach, "far_list": far_list, "slopes": slopes}


def block_attention(query_rows, key_part, value_part, key_pos, key_mask, query_pos, slopes):
    head_count = slopes.shape[0]
    head_size = query_rows.shape[1] // head_count
    queries_h = query_rows.astype(jnp.float32).reshape(query_rows.shape[0], head_count, head_size)
    keys_h = key_part.astype(jnp.float32).reshape(key_part.shape[0], head_count, head_size)
    values_h = value_part.astype(jnp.float32).reshape(value_part.shape[0], head_count, head_size)
    scores = jnp.einsum('qhd,khd->hqk', queries_h, keys_h) * (1.0 / math.sqrt(head_size))
    distance = jnp.abs(query_pos[:, None] - key_pos[None, :]).astype(jnp.float32)
    scores = scores - slopes[:, None, None] * distance[None, :, :]
    scores = jnp.where(key_mask[None, None, :], scores, -jnp.inf)
    row_max = lax.optimization_barrier(jnp.max(scores, axis=2, keepdims=True))
    raised = jnp.exp(scores - row_max)
    weights = (raised / lax.optimization_barrier(jnp.sum(raised, axis=2, keepdims=True))).astype(jnp.bfloat16)
    attended = jnp.einsum('hqk,khd->qhd', weights.astype(jnp.float32), values_h)
    return attended.astype(jnp.bfloat16).reshape(query_rows.shape[0], head_count * head_size)

def reference(queries, key_rows, value_rows, band_reach, far_list, slopes):
    total_tokens, channels = key_rows.shape
    total_blocks = total_tokens // BT
    margin = BAND * BT
    band_span = 2 * BAND + 1
    keys_pad = jnp.pad(key_rows, ((margin, margin), (0, 0)))
    values_pad = jnp.pad(value_rows, ((margin, margin), (0, 0)))
    offsets = jnp.arange(band_span, dtype=jnp.int32) - BAND
    within = jnp.arange(BT, dtype=jnp.int32)

    def attend(block_id):
        first_row = block_id * BT
        band_keys = lax.dynamic_slice_in_dim(keys_pad, first_row, band_span * BT, 0)
        band_values = lax.dynamic_slice_in_dim(values_pad, first_row, band_span * BT, 0)
        far_here = far_list[block_id]
        far_keys = jnp.concatenate([lax.dynamic_slice_in_dim(key_rows, (far_here[far_slot] * BT).astype(jnp.int32), BT, 0) for far_slot in range(FAR)], axis=0)
        far_values = jnp.concatenate([lax.dynamic_slice_in_dim(value_rows, (far_here[far_slot] * BT).astype(jnp.int32), BT, 0) for far_slot in range(FAR)], axis=0)
        band_blocks = block_id + offsets
        band_ok = (jnp.abs(offsets) <= band_reach[block_id]) & (band_blocks >= 0) & (band_blocks < total_blocks)
        key_blocks = jnp.concatenate([band_blocks, far_here.astype(jnp.int32)])
        key_ok = jnp.concatenate([band_ok, jnp.ones((FAR,), jnp.bool_)])
        key_pos = (key_blocks[:, None] * BT + within[None, :]).reshape(-1)
        key_mask = jnp.repeat(key_ok, BT)
        query_rows = lax.dynamic_slice_in_dim(queries, first_row, BT, 0)
        return block_attention(query_rows, jnp.concatenate([band_keys, far_keys], axis=0), jnp.concatenate([band_values, far_values], axis=0), key_pos, key_mask, first_row + within, slopes)
    attended = lax.map(attend, jnp.arange(total_blocks, dtype=jnp.int32))
    return attended.reshape(total_tokens, channels)
```

```python
import functools
import math

import jax
import jax.numpy as jnp
from jax import lax
from jax.experimental import pallas as pl
from jax.experimental.pallas import tpu as pltpu
from jax.sharding import PartitionSpec as P

BT = 256
BAND = 3
FAR = 2
DH = 128
LOG2E = math.log2(math.e)
SCALE = LOG2E / math.sqrt(DH)
LOW = -1e30
VMEM = 56 * 2**20


def params():
    return pltpu.CompilerParams(vmem_limit_bytes=VMEM, dimension_semantics=("arbitrary",))


def pack_kernel(asked, k_ref, v_ref, out_ref):
    out_ref[0, 0] = k_ref[...]
    out_ref[0, 1] = v_ref[...]


def pack(asked, keys, values, start, width):
    slots = asked.shape[0]
    at = start // width
    spec = pl.BlockSpec((BT, width), lambda s, asked: (asked[s], at))
    return pl.pallas_call(
        pack_kernel,
        grid_spec=pltpu.PrefetchScalarGridSpec(
            num_scalar_prefetch=1,
            grid=(slots,),
            in_specs=[spec, spec],
            out_specs=pl.BlockSpec((1, 2, BT, width), lambda s, asked: (s, 0, 0, 0)),
        ),
        out_shape=jax.ShapeDtypeStruct((slots, 2, BT, width), keys.dtype),
        compiler_params=params(),
        cost_estimate=pl.CostEstimate(flops=0, bytes_accessed=slots * BT * width * 8, transcendentals=0),
        name="pack",
    )(asked, keys, values)


def distances(gap):
    rows = lax.broadcasted_iota(jnp.int32, (BT, BT), 0)
    cols = lax.broadcasted_iota(jnp.int32, (BT, BT), 1)
    return jnp.abs(rows - cols + gap).astype(jnp.float32)


def visit(heads, slopes, gap, query, key, value, top, total, acc):
    far = distances(gap)
    for h in range(heads):
        lanes = slice(h * DH, (h + 1) * DH)
        s = lax.dot_general(query(lanes), key(lanes), (((1,), (1,)), ((), ())), preferred_element_type=jnp.float32)
        s = s * SCALE - slopes(h) * far
        old = top[h]
        new = jnp.maximum(old, jnp.max(s, axis=1, keepdims=True))
        p = jnp.exp2(s - new)
        shrink = jnp.exp2(old - new)
        top[h] = new
        total[h] = total[h] * shrink + jnp.sum(p, axis=1, keepdims=True)
        acc[:, lanes] = acc[:, lanes] * shrink + jnp.dot(
            p.astype(jnp.bfloat16), value(lanes), preferred_element_type=jnp.float32
        )


def near_kernel(n, heads, reach, slopes, q_ref, k_ref, v_ref, acc, stats, top, total):
    i = pl.program_id(0)
    top[...] = jnp.full_like(top, LOW)
    total[...] = jnp.zeros_like(total)
    acc[...] = jnp.zeros_like(acc)
    wide = reach[i]

    def step(j, carry):
        rows = pl.ds(pl.multiple_of(j * BT, BT), BT)
        visit(
            heads, lambda h: slopes[h], (i - j) * BT,
            lambda c: q_ref[:, c], lambda c: k_ref[rows, c], lambda c: v_ref[rows, c],
            top, total, acc,
        )
        return carry

    lax.fori_loop(jnp.maximum(i - wide, 0), jnp.minimum(i + wide, n - 1) + 1, step, 0)
    lane = lax.broadcasted_iota(jnp.int32, (BT, DH), 1)
    kept = jnp.zeros((BT, DH), jnp.float32)
    for h in range(heads):
        kept = jnp.where(lane == 2 * h, top[h], kept)
        kept = jnp.where(lane == 2 * h + 1, total[h], kept)
    stats[...] = kept


def near(reach, slopes, queries, keys, values):
    rows, channels = keys.shape
    n, heads = rows // BT, channels // DH
    block = pl.BlockSpec((BT, channels), lambda i, *_: (i, 0))
    whole = pl.BlockSpec((rows, channels), lambda i, *_: (0, 0))
    return pl.pallas_call(
        functools.partial(near_kernel, n, heads),
        grid_spec=pltpu.PrefetchScalarGridSpec(
            num_scalar_prefetch=2,
            grid=(n,),
            in_specs=[block, whole, whole],
            out_specs=[block, pl.BlockSpec((BT, DH), lambda i, *_: (i, 0))],
            scratch_shapes=[pltpu.VMEM((heads, BT, 1), jnp.float32)] * 2,
        ),
        out_shape=[
            jax.ShapeDtypeStruct((rows, channels), jnp.float32),
            jax.ShapeDtypeStruct((rows, DH), jnp.float32),
        ],
        compiler_params=params(),
        cost_estimate=pl.CostEstimate(
            flops=rows * 7 * BT * channels * 16, bytes_accessed=rows * channels * 12, transcendentals=rows * 7 * BT * heads
        ),
        name="near",
    )(reach, slopes, queries, keys, values)


def rest_kernel(
    n, heads, first, reach, info, far_list, slot, slopes,
    q_ref, acc_ref, stats_ref, kp, vp, kn, vn, far0, far1, out_ref, top, total, acc,
):
    i = pl.program_id(0)
    me, last = info[0], info[1]
    wide = reach[i]
    acc[...] = acc_ref[...]
    for h in range(heads):
        at = 2 * (first + h)
        top[h] = stats_ref[:, at : at + 1]
        total[h] = stats_ref[:, at + 1 : at + 2]

    def beside(k_ref, v_ref, offset):
        def step(b, carry):
            rows = pl.ds(pl.multiple_of(b * BT, BT), BT)
            visit(
                heads, lambda h: slopes[first + h], (i - offset - b) * BT,
                lambda c: q_ref[:, c], lambda c: k_ref[rows, c], lambda c: v_ref[rows, c],
                top, total, acc,
            )
            return carry

        return step

    lax.fori_loop(jnp.where(me == 0, BAND, jnp.minimum(i + BAND - wide, BAND)), BAND, beside(kp, vp, -BAND), 0)
    lax.fori_loop(0, jnp.where(me == last, 0, jnp.maximum(i + wide + 1 - n, 0)), beside(kn, vn, n), 0)
    for f, ref in enumerate((far0, far1)):
        visit(
            heads, lambda h: slopes[first + h], (me * n + i - far_list[FAR * i + f]) * BT,
            lambda c: q_ref[:, c], lambda c: ref[0, 0, :, c], lambda c: ref[0, 1, :, c],
            top, total, acc,
        )
    for h in range(heads):
        lanes = slice(h * DH, (h + 1) * DH)
        out_ref[:, lanes] = (acc[:, lanes] / total[h]).astype(out_ref.dtype)


def rest(reach, info, far_list, slot, slopes, queries, acc, stats, halos, incoming, start, width):
    rows = queries.shape[0]
    n, heads, at = rows // BT, width // DH, start // width
    block = pl.BlockSpec((BT, width), lambda i, *_: (i, at))
    halo = pl.BlockSpec((BAND * BT, width), lambda i, *_: (0, at))

    def far(f):
        return pl.BlockSpec((1, 2, BT, width), lambda i, reach, info, far_list, slot, slopes: (slot[FAR * i + f], 0, 0, 0))

    return pl.pallas_call(
        functools.partial(rest_kernel, n, heads, start // DH),
        grid_spec=pltpu.PrefetchScalarGridSpec(
            num_scalar_prefetch=5,
            grid=(n,),
            in_specs=[block, block, pl.BlockSpec((BT, DH), lambda i, *_: (i, 0)), halo, halo, halo, halo, far(0), far(1)],
            out_specs=pl.BlockSpec((BT, width), lambda i, *_: (i, 0)),
            scratch_shapes=[pltpu.VMEM((heads, BT, 1), jnp.float32)] * 2 + [pltpu.VMEM((BT, width), jnp.float32)],
        ),
        out_shape=jax.ShapeDtypeStruct((rows, width), queries.dtype),
        compiler_params=params(),
        cost_estimate=pl.CostEstimate(
            flops=rows * 3 * BT * width * 16, bytes_accessed=rows * width * 16, transcendentals=rows * 3 * BT * heads
        ),
        name="rest",
    )(reach, info, far_list, slot, slopes, queries, acc, stats, *halos, incoming, incoming)


def join_kernel(widths, sources, order, *refs):
    out_ref, at, channels = refs[-1], 0, sum(widths)
    for c, width in enumerate(widths):
        for k in range(sources):
            column = pl.multiple_of(order[k] * channels + at, math.gcd(channels, at))
            out_ref[:, pl.ds(column, width)] = refs[c * sources + k][...]
        at += width


def join(order, chunks):
    sources, rows = len(chunks[0]), chunks[0][0].shape[0]
    tile = math.gcd(rows, 128)
    parts = [part for chunk in chunks for part in chunk]
    widths = [chunk[0].shape[1] for chunk in chunks]
    channels = sources * sum(widths)
    return pl.pallas_call(
        functools.partial(join_kernel, widths, sources),
        grid_spec=pltpu.PrefetchScalarGridSpec(
            num_scalar_prefetch=1,
            grid=(rows // tile,),
            in_specs=[pl.BlockSpec((tile, part.shape[1]), lambda r, order: (r, 0)) for part in parts],
            out_specs=pl.BlockSpec((tile, channels), lambda r, order: (r, 0)),
        ),
        out_shape=jax.ShapeDtypeStruct((rows, channels), parts[0].dtype),
        compiler_params=params(),
        name="join",
    )(order, *parts)


def body(queries, key_rows, value_rows, band_reach, far_list, slopes):
    me = lax.axis_index("seq")
    size, head_size = lax.axis_size("seq"), lax.axis_size("head")
    tok_rows, channels = key_rows.shape
    blk_dev, heads = tok_rows // BT, channels // DH
    margin = BAND * BT
    requests = far_list.reshape(-1)
    capacity = max(2, -(-requests.shape[0] // size))
    source = requests // blk_dev
    local_blk = requests % blk_dev
    order = jnp.arange(requests.shape[0])
    earlier = (source[:, None] == source[None, :]) & (order[None, :] < order[:, None])
    rank = jnp.sum(earlier.astype(jnp.int32), axis=1)
    slot = source * capacity + rank
    placed = slot[:, None] == jnp.arange(size * capacity)[None, :]
    table = jnp.sum(jnp.where(placed, local_blk[:, None], 0), axis=0)
    asked = lax.all_to_all(table.reshape(size, capacity), "seq", split_axis=0, concat_axis=0, tiled=True).reshape(-1)
    up = [(i, i + 1) for i in range(size - 1)]
    down = [(j, i) for i, j in up]
    info = jnp.stack([me, jnp.full_like(me, size - 1)]).astype(jnp.int32)
    steep = slopes * LOG2E

    last = heads // 4 if heads % 4 == 0 else heads // 2
    chunks = [(0, channels - last * DH), (channels - last * DH, last * DH)]
    halos = (
        lax.ppermute(key_rows[-margin:], "seq", up),
        lax.ppermute(value_rows[-margin:], "seq", up),
        lax.ppermute(key_rows[:margin], "seq", down),
        lax.ppermute(value_rows[:margin], "seq", down),
    )
    first = pack(asked, key_rows, value_rows, *chunks[0])

    def exchange(packed):
        shape = packed.shape
        packed = packed.reshape(size, capacity, *shape[1:])
        return lax.all_to_all(packed, "seq", split_axis=0, concat_axis=0, tiled=True).reshape(shape)

    arrived = exchange(first)
    second = pack(asked, key_rows, value_rows, *chunks[1])
    acc, stats = near(band_reach, steep, queries, key_rows, value_rows)
    arrived, second, acc, stats, halos = lax.optimization_barrier((arrived, second, acc, stats, halos))
    arrived2 = exchange(second)
    place = lax.axis_index("head")

    def turn(part):
        own = tok_rows // head_size
        got = []
        for k in range(head_size):
            rows = lax.dynamic_slice_in_dim(part, lax.rem(place + k, head_size) * own, own, 0)
            got.append(rows if k == 0 else lax.ppermute(rows, "head", [(i, (i + k) % head_size) for i in range(head_size)]))
        return got

    def finish(far, chunk):
        return turn(rest(band_reach, info, requests, slot, steep, queries, acc, stats, halos, far, *chunk))

    order = lax.rem(place + head_size - jnp.arange(head_size, dtype=jnp.int32), head_size)
    return join(order, [finish(arrived, chunks[0]), finish(arrived2, chunks[1])])


def solution(mesh):
    in_specs = (
        P("seq", "head"),
        P("seq", "head"),
        P("seq", "head"),
        P("seq"),
        P("seq", None),
        P("head"),
    )
    out_specs = P(("seq", "head"), None)
    return jax.shard_map(body, mesh=mesh, in_specs=in_specs, out_specs=out_specs, check_vma=False)
```

```python
import functools
import math

import jax
import jax.numpy as jnp
from jax import lax
from jax.experimental import pallas as pl
from jax.experimental.pallas import tpu as pltpu
from jax.sharding import PartitionSpec as P

BT = 256
BAND = 3
FAR = 2
DH = 128
LOG2E = math.log2(math.e)
SCALE = LOG2E / math.sqrt(DH)
LOW = -1e30
VMEM = 56 * 2**20


def params():
    return pltpu.CompilerParams(vmem_limit_bytes=VMEM, dimension_semantics=("arbitrary",))


def pack_kernel(asked, k_ref, v_ref, out_ref):
    out_ref[0, 0] = k_ref[...]
    out_ref[0, 1] = v_ref[...]


def pack(asked, keys, values, start, width):
    slots = asked.shape[0]
    at = start // width
    spec = pl.BlockSpec((BT, width), lambda s, asked: (asked[s], at))
    return pl.pallas_call(
        pack_kernel,
        grid_spec=pltpu.PrefetchScalarGridSpec(
            num_scalar_prefetch=1,
            grid=(slots,),
            in_specs=[spec, spec],
            out_specs=pl.BlockSpec((1, 2, BT, width), lambda s, asked: (s, 0, 0, 0)),
        ),
        out_shape=jax.ShapeDtypeStruct((slots, 2, BT, width), keys.dtype),
        compiler_params=params(),
        cost_estimate=pl.CostEstimate(flops=0, bytes_accessed=slots * BT * width * 8, transcendentals=0),
        name="pack",
    )(asked, keys, values)


def distances(gap):
    rows = lax.broadcasted_iota(jnp.int32, (BT, BT), 0)
    cols = lax.broadcasted_iota(jnp.int32, (BT, BT), 1)
    return jnp.abs(rows - cols + gap).astype(jnp.float32)


def visit(heads, slopes, query, blocks, top, acc):
    fars = [distances(gap) for gap, _, _ in blocks]
    ones = jnp.ones((BT, DH), jnp.bfloat16)
    for h in range(heads):
        lanes = slice(h * DH, (h + 1) * DH)
        scores = [
            lax.dot_general(query(lanes), key(lanes), (((1,), (1,)), ((), ())), preferred_element_type=jnp.float32) * SCALE
            - slopes(h) * far
            for far, (_, key, _) in zip(fars, blocks)
        ]
        old = top[h]
        new = jnp.maximum(old, jnp.max(functools.reduce(jnp.maximum, scores), axis=1, keepdims=True))
        top[h] = new
        summed = acc[h] * jnp.exp2(old - new)
        for s, (_, _, value) in zip(scores, blocks):
            p = jnp.exp2(s - new).astype(jnp.bfloat16)
            both = jnp.concatenate([value(lanes), ones], axis=1)
            summed = summed + jnp.dot(p, both, preferred_element_type=jnp.float32)
        acc[h] = summed


def near_kernel(n, heads, reach, slopes, q_ref, k_ref, v_ref, acc_ref, stats, top, acc):
    i = pl.program_id(0)
    top[...] = jnp.full_like(top, LOW)
    acc[...] = jnp.zeros_like(acc)
    wide = reach[i]

    def step(j, carry):
        rows = pl.ds(pl.multiple_of(j * BT, BT), BT)
        visit(
            heads, lambda h: slopes[h], lambda c: q_ref[:, c],
            [((i - j) * BT, lambda c: k_ref[rows, c], lambda c: v_ref[rows, c])], top, acc,
        )
        return carry

    lax.fori_loop(jnp.maximum(i - wide, 0), jnp.minimum(i + wide, n - 1) + 1, step, 0)
    lane = lax.broadcasted_iota(jnp.int32, (BT, DH), 1)
    kept = jnp.zeros((BT, DH), jnp.float32)
    for h in range(heads):
        kept = jnp.where(lane == 2 * h, top[h], kept)
        kept = jnp.where(lane == 2 * h + 1, acc[h, :, DH:], kept)
        acc_ref[:, h * DH : (h + 1) * DH] = acc[h, :, :DH]
    stats[...] = kept


def near(reach, slopes, queries, keys, values):
    rows, channels = keys.shape
    n, heads = rows // BT, channels // DH
    block = pl.BlockSpec((BT, channels), lambda i, *_: (i, 0))
    whole = pl.BlockSpec((rows, channels), lambda i, *_: (0, 0))
    return pl.pallas_call(
        functools.partial(near_kernel, n, heads),
        grid_spec=pltpu.PrefetchScalarGridSpec(
            num_scalar_prefetch=2,
            grid=(n,),
            in_specs=[block, whole, whole],
            out_specs=[block, pl.BlockSpec((BT, DH), lambda i, *_: (i, 0))],
            scratch_shapes=[pltpu.VMEM((heads, BT, 1), jnp.float32), pltpu.VMEM((heads, BT, 2 * DH), jnp.float32)],
        ),
        out_shape=[
            jax.ShapeDtypeStruct((rows, channels), jnp.float32),
            jax.ShapeDtypeStruct((rows, DH), jnp.float32),
        ],
        compiler_params=params(),
        cost_estimate=pl.CostEstimate(
            flops=rows * 7 * BT * channels * 16, bytes_accessed=rows * channels * 12, transcendentals=rows * 7 * BT * heads
        ),
        name="near",
    )(reach, slopes, queries, keys, values)


def rest_kernel(
    n, heads, first, reach, info, far_list, slot, slopes,
    q_ref, acc_ref, stats_ref, kp, vp, kn, vn, far0, far1, out_ref, top, acc,
):
    i = pl.program_id(0)
    me, last = info[0], info[1]
    wide = reach[i]
    for h in range(heads):
        at = 2 * (first + h)
        top[h] = stats_ref[:, at : at + 1]
        acc[h, :, :DH] = acc_ref[:, h * DH : (h + 1) * DH]
        acc[h, :, DH:] = jnp.broadcast_to(stats_ref[:, at + 1 : at + 2], (BT, DH))

    def beside(k_ref, v_ref, offset):
        def step(b, carry):
            rows = pl.ds(pl.multiple_of(b * BT, BT), BT)
            visit(
                heads, lambda h: slopes[first + h], lambda c: q_ref[:, c],
                [((i - offset - b) * BT, lambda c: k_ref[rows, c], lambda c: v_ref[rows, c])], top, acc,
            )
            return carry

        return step

    lax.fori_loop(jnp.where(me == 0, BAND, jnp.minimum(i + BAND - wide, BAND)), BAND, beside(kp, vp, -BAND), 0)
    lax.fori_loop(0, jnp.where(me == last, 0, jnp.maximum(i + wide + 1 - n, 0)), beside(kn, vn, n), 0)
    listed = [
        ((me * n + i - far_list[FAR * i + f]) * BT, lambda c, ref=ref: ref[0, 0, :, c], lambda c, ref=ref: ref[0, 1, :, c])
        for f, ref in enumerate((far0, far1))
    ]
    visit(heads, lambda h: slopes[first + h], lambda c: q_ref[:, c], listed, top, acc)
    for h in range(heads):
        out_ref[:, h * DH : (h + 1) * DH] = (acc[h, :, :DH] / acc[h, :, DH:]).astype(out_ref.dtype)


def rest(reach, info, far_list, slot, slopes, queries, acc, stats, halos, incoming, start, width):
    rows = queries.shape[0]
    n, heads, at = rows // BT, width // DH, start // width
    block = pl.BlockSpec((BT, width), lambda i, *_: (i, at))
    halo = pl.BlockSpec((BAND * BT, width), lambda i, *_: (0, at))

    def far(f):
        return pl.BlockSpec((1, 2, BT, width), lambda i, reach, info, far_list, slot, slopes: (slot[FAR * i + f], 0, 0, 0))

    return pl.pallas_call(
        functools.partial(rest_kernel, n, heads, start // DH),
        grid_spec=pltpu.PrefetchScalarGridSpec(
            num_scalar_prefetch=5,
            grid=(n,),
            in_specs=[block, block, pl.BlockSpec((BT, DH), lambda i, *_: (i, 0)), halo, halo, halo, halo, far(0), far(1)],
            out_specs=pl.BlockSpec((BT, width), lambda i, *_: (i, 0)),
            scratch_shapes=[pltpu.VMEM((heads, BT, 1), jnp.float32), pltpu.VMEM((heads, BT, 2 * DH), jnp.float32)],
        ),
        out_shape=jax.ShapeDtypeStruct((rows, width), queries.dtype),
        compiler_params=params(),
        cost_estimate=pl.CostEstimate(
            flops=rows * 3 * BT * width * 16, bytes_accessed=rows * width * 16, transcendentals=rows * 3 * BT * heads
        ),
        name="rest",
    )(reach, info, far_list, slot, slopes, queries, acc, stats, *halos, incoming, incoming)


def join_kernel(widths, sources, order, *refs):
    out_ref, at, channels = refs[-1], 0, sum(widths)
    for c, width in enumerate(widths):
        for k in range(sources):
            column = pl.multiple_of(order[k] * channels + at, math.gcd(channels, at))
            out_ref[:, pl.ds(column, width)] = refs[c * sources + k][...]
        at += width


def join(order, chunks):
    sources, rows = len(chunks[0]), chunks[0][0].shape[0]
    tile = math.gcd(rows, 128)
    parts = [part for chunk in chunks for part in chunk]
    widths = [chunk[0].shape[1] for chunk in chunks]
    channels = sources * sum(widths)
    return pl.pallas_call(
        functools.partial(join_kernel, widths, sources),
        grid_spec=pltpu.PrefetchScalarGridSpec(
            num_scalar_prefetch=1,
            grid=(rows // tile,),
            in_specs=[pl.BlockSpec((tile, part.shape[1]), lambda r, order: (r, 0)) for part in parts],
            out_specs=pl.BlockSpec((tile, channels), lambda r, order: (r, 0)),
        ),
        out_shape=jax.ShapeDtypeStruct((rows, channels), parts[0].dtype),
        compiler_params=params(),
        name="join",
    )(order, *parts)


def body(queries, key_rows, value_rows, band_reach, far_list, slopes):
    me = lax.axis_index("seq")
    size, head_size = lax.axis_size("seq"), lax.axis_size("head")
    tok_rows, channels = key_rows.shape
    blk_dev, heads = tok_rows // BT, channels // DH
    margin = BAND * BT
    requests = far_list.reshape(-1)
    capacity = max(2, -(-requests.shape[0] // size))
    source = requests // blk_dev
    local_blk = requests % blk_dev
    order = jnp.arange(requests.shape[0])
    earlier = (source[:, None] == source[None, :]) & (order[None, :] < order[:, None])
    rank = jnp.sum(earlier.astype(jnp.int32), axis=1)
    slot = source * capacity + rank
    placed = slot[:, None] == jnp.arange(size * capacity)[None, :]
    table = jnp.sum(jnp.where(placed, local_blk[:, None], 0), axis=0)
    asked = lax.all_to_all(table.reshape(size, capacity), "seq", split_axis=0, concat_axis=0, tiled=True).reshape(-1)
    up = [(i, i + 1) for i in range(size - 1)]
    down = [(j, i) for i, j in up]
    info = jnp.stack([me, jnp.full_like(me, size - 1)]).astype(jnp.int32)
    steep = slopes * LOG2E

    most = max(heads - 2, 1)
    chunks = [(0, most * DH)] + [(h * DH, DH) for h in range(most, heads)]
    halos = (
        lax.ppermute(key_rows[-margin:], "seq", up),
        lax.ppermute(value_rows[-margin:], "seq", up),
        lax.ppermute(key_rows[:margin], "seq", down),
        lax.ppermute(value_rows[:margin], "seq", down),
    )
    packed = [pack(asked, key_rows, value_rows, *chunk) for chunk in chunks]
    packed[0], *keys_beside = lax.optimization_barrier((packed[0], halos[0], halos[2]))

    def exchange(packed):
        shape = packed.shape
        blocks = packed.reshape(size, capacity, *shape[1:])
        return lax.all_to_all(blocks, "seq", split_axis=0, concat_axis=0, tiled=True).reshape(shape)

    acc, stats = near(band_reach, steep, queries, key_rows, value_rows)
    arrived = [exchange(packed[0])]
    halos = (keys_beside[0], halos[1], keys_beside[1], halos[3])

    def finish(later):
        return rest(
            band_reach, info, requests, slot, steep, queries, acc, stats, halos, arrived[later], *chunks[later]
        )

    done = []
    for later in range(1, len(chunks)):
        if later > 1:
            done.append(finish(later - 2))
        arrived[-1], packed[later], acc, stats, halos, done = lax.optimization_barrier(
            (arrived[-1], packed[later], acc, stats, halos, done)
        )
        arrived.append(exchange(packed[later]))
    done += [finish(later) for later in range(len(done), len(chunks))]
    place = lax.axis_index("head")

    def turn(part):
        own = tok_rows // head_size
        got = []
        for k in range(head_size):
            rows = lax.dynamic_slice_in_dim(part, lax.rem(place + k, head_size) * own, own, 0)
            got.append(rows if k == 0 else lax.ppermute(rows, "head", [(i, (i + k) % head_size) for i in range(head_size)]))
        return got

    order = lax.rem(place + head_size - jnp.arange(head_size, dtype=jnp.int32), head_size)
    return join(order, [turn(part) for part in done])


def solution(mesh):
    in_specs = (
        P("seq", "head"),
        P("seq", "head"),
        P("seq", "head"),
        P("seq"),
        P("seq", None),
        P("head"),
    )
    out_specs = P(("seq", "head"), None)
    return jax.shard_map(body, mesh=mesh, in_specs=in_specs, out_specs=out_specs, check_vma=False)
```
